32 devices in a mesh: seq: 16 (over z, y, x), head: 2 (over core).
Axes of the slice: x: 2, y: 2, z: 4, core: 2. Of those that a mesh axis runs over, the one named last changes fastest.
Arguments:
- queries: bfloat16 [4096, 5120], P('seq', 'head'), may hold values from -12 to 12
- keys: bfloat16 [4096, 5120], P('seq', 'head'), may hold values from -4.5 to 4.5
- values: bfloat16 [4096, 5120], P('seq', 'head'), may hold values from -6 to 6
- class_map: int32 [40, 32, 8, 2], P('head', 'seq'), may hold values from 0 to 2, as said below
- out_weight: bfloat16 [5120, 5120], P('seq', 'head'), may hold values from -0.5 to 0.5
Outputs:
- mixed: bfloat16 [4096, 5120], P(('seq', 'head'))
The draws below stay inside these ranges and needn't reach their ends.
Inputs may be any that keep to these rules, and one draw needn't show every extreme that they name: `class_map`: entry [h, b, r, j] classes, for head h, the pair of query block b and key block j of the token shard r places before block b's shard, counted cyclically (0 skipped, 1 linear, 2 exact softmax). Every query block's own key block (r = 0, j = b mod 2) is 2.
All inputs are finite; a program needn't handle non-finite values.
Results may differ from the reference program's by a relative error of at most 0.0061.
Values may be sent and summed in bfloat16 or wider, within the bound.
No kernel may reach another device: no remote copies, remote signals or barrier semaphores. Data moves between devices by JAX's collectives and lax.ppermute only.
A program may use at most 256 MiB of HBM per device.

```python
import math
import jax
import jax.numpy as jnp
from jax import lax

D = 5120
HEADS = 40
HD = 128
TOK_DEV = 256
BLOCK = 128
CYCLE = 8
BLK_DEV = 2
TOKENS = 4096
QBLOCKS = 32
N_SEQ = 16
N_HEAD = 2


def draw_queries(key, part):
    key = jax.random.fold_in(key, 21)
    key_values, key_scale = jax.random.split(key)
    row_scale = jnp.exp(jax.random.uniform(key_scale, (TOKENS, HEADS, 1), jnp.float32, math.log(0.3), math.log(3.0)))
    base_values = jnp.clip(jax.random.normal(key_values, (TOKENS, HEADS, HD), jnp.float32), -4.0, 4.0) * row_scale
    return base_values.reshape(TOKENS, HEADS * HD).astype(jnp.bfloat16)


def draw_keys(key, part):
    key = jax.random.fold_in(key, 22)
    base_values = jnp.clip(jax.random.normal(key, (TOKENS, HEADS, HD), jnp.float32), -4.0, 4.0)
    return base_values.reshape(TOKENS, HEADS * HD).astype(jnp.bfloat16)


def draw_class_map(key, part):
    key = jax.random.fold_in(key, 23)
    key_density, key_ticket = jax.random.split(key)
    density = jax.random.randint(key_density, (1, QBLOCKS, 1, 1), 0, 5)
    ticket = jax.random.randint(key_ticket, (HEADS, QBLOCKS, CYCLE, BLK_DEV), 0, 8)
    classes = jnp.where(ticket < 2 * density, 2, jnp.where(ticket < 2 * density + 4, 1, 0))
    own_offset = jnp.arange(CYCLE)[None, None, :, None] == 0
    own_block = jnp.arange(BLK_DEV)[None, None, None, :] == (jnp.arange(QBLOCKS) % BLK_DEV)[None, :, None, None]
    return jnp.where(own_offset & own_block, 2, classes).astype(jnp.int32)


def levels(own_key, extent, shards, least, largest):
    def one(dim, blocks):
        draws = jax.random.uniform(jax.random.fold_in(jax.random.fold_in(own_key, 6), dim), (blocks,), jnp.float32, least / len(shards), largest / len(shards))
        return jnp.repeat(jnp.exp(draws), extent[dim] // blocks).reshape((-1,) + (1,) * (len(extent) - dim - 1))

    level = one(*shards[0])
    for cut in shards[1:]:
        level = level * one(*cut)
    return level


def bell_draw(rng, dims, scale, limit, shards=(), kind=jnp.bfloat16):
    loudness = levels(rng, dims, shards, -0.22, 0.18) if shards else 1.0
    values = jax.random.normal(rng, dims, jnp.float32) * scale * loudness
    return jnp.minimum(jnp.maximum(values, -limit), limit).astype(kind)


def setup_inputs(seed: int = 0) -> dict:
    splits = jax.random.split(jax.random.key(seed), 6)
    queries = draw_queries(jax.random.fold_in(splits[5], 71), 0)
    keys = draw_keys(jax.random.fold_in(splits[5], 71), 0)
    values = bell_draw(splits[2], (TOKENS, HEADS * HD), 1.0, 6.0, ((0, 16), (1, 2)))
    class_map = draw_class_map(jax.random.fold_in(splits[5], 71), 0)
    out_weight = bell_draw(splits[4], (D, HEADS * HD), HD ** -0.5, 0.5, ((0, 16), (1, 2)))
    return dict(queries=queries, keys=keys, values=values, class_map=class_map, out_weight=out_weight)


def round_bf16(numbers):
    return lax.optimization_barrier(numbers.astype(jnp.bfloat16)).astype(jnp.float32)

def features_of(numbers):
    return round_bf16(jax.nn.elu(numbers) + 1.0)

def one_head(operands):
    query_head, key_head, value_head, class_head = operands
    offsets = ((jnp.arange(N_SEQ)[:, None] - jnp.arange(CYCLE)[None, :]) % N_SEQ).astype(jnp.int32)
    key_shards = key_head.astype(jnp.float32).reshape(N_SEQ, TOK_DEV, HD)
    value_shards = value_head.astype(jnp.float32).reshape(N_SEQ, TOK_DEV, HD)
    key_window = jnp.take(key_shards, offsets, axis=0).reshape(N_SEQ, CYCLE * TOK_DEV, HD)
    value_window = jnp.take(value_shards, offsets, axis=0).reshape(N_SEQ, CYCLE * TOK_DEV, HD)
    query_shards = query_head.astype(jnp.float32).reshape(N_SEQ, TOK_DEV, HD)
    block_classes = class_head.reshape(N_SEQ, BLK_DEV, CYCLE, BLK_DEV)
    classes = jnp.broadcast_to(block_classes[:, :, None, :, :, None], (N_SEQ, BLK_DEV, BLOCK, CYCLE, BLK_DEV, BLOCK))
    classes = classes.reshape(N_SEQ, TOK_DEV, CYCLE * TOK_DEV)
    scores = jnp.einsum('std,sud->stu', query_shards, key_window) * (1.0 / math.sqrt(HD))
    masked = jnp.where(classes == 2, scores, -jnp.inf)
    row_max = lax.optimization_barrier(jnp.max(masked, axis=2, keepdims=True))
    probs = jnp.exp(masked - row_max)
    exact_total = lax.optimization_barrier(jnp.sum(probs, axis=2, keepdims=True))
    exact_out = jnp.einsum('stu,sud->std', round_bf16(probs), value_window) / exact_total
    affinity = jnp.einsum('std,sud->stu', features_of(query_shards), features_of(key_window))
    affinity = jnp.where(classes == 1, affinity, 0.0)
    linear_total = jnp.maximum(lax.optimization_barrier(jnp.sum(affinity, axis=2, keepdims=True)), 1.0)
    linear_out = jnp.einsum('stu,sud->std', round_bf16(affinity), value_window) / linear_total
    return (exact_out + linear_out).reshape(TOKENS, HD)

def by_head(array):
    return array.reshape(TOKENS, HEADS, HD).transpose(1, 0, 2)

def reference(queries, keys, values, class_map, out_weight):
    heads_out = lax.map(one_head, (by_head(queries), by_head(keys), by_head(values), class_map))
    attended = heads_out.transpose(1, 0, 2).reshape(TOKENS, HEADS * HD).astype(jnp.bfloat16)
    group_width = HEADS * HD // N_HEAD
    mixed = jnp.zeros((TOKENS, D), jnp.float32)
    for group_index in range(N_HEAD):
        first_col = group_index * group_width
        last_col = first_col + group_width
        group_part = jnp.dot(attended[:, first_col:last_col], out_weight[:, first_col:last_col].T, preferred_element_type=jnp.float32)
        mixed = mixed + round_bf16(group_part)
    return mixed.astype(jnp.bfloat16)
```

```python
import functools
import math

import jax
import jax.numpy as jnp
from jax import lax
from jax.experimental import pallas as pl
from jax.experimental.pallas import tpu as pltpu
from jax.sharding import PartitionSpec as P

HD = 128
CYCLE = 8
BLOCK = 128
LINE = 4
PLANE = 4
CHUNKS = (2, 3)
MASKED = -1e30


def feature_map(numbers):
    x = numbers.astype(jnp.float32)
    return jnp.where(x > 0, x + 1.0, jnp.exp(jnp.minimum(x, 0.0))).astype(jnp.bfloat16)


def passed_along(value, axis, steps):
    count = lax.axis_size(axis)
    pairs = [(source, (source + steps) % count) for source in range(count)]
    return lax.ppermute(value, axis, pairs)


def token_classes(block_row, tok_rows, key_rows):
    heads_here, query_blocks, key_blocks = block_row.shape
    query_width = tok_rows // query_blocks
    key_width = key_rows // key_blocks
    widened = jnp.broadcast_to(
        block_row[:, :, None, :, None],
        (heads_here, query_blocks, query_width, key_blocks, key_width),
    )
    return widened.reshape(heads_here, tok_rows, key_rows)


def ring_plan(queries, keys, values, class_map, out_weight):
    tok_rows = queries.shape[0]
    heads_here = queries.shape[1] // HD
    current = jnp.stack([keys, values])
    arrivals = [current]
    for _ in range(1, CYCLE):
        current = passed_along(current, "seq", 1)
        arrivals.append(current)
    window = jnp.concatenate(arrivals, axis=1)
    key_rows = window.shape[1]
    query_heads = queries.reshape(tok_rows, heads_here, HD)
    key_heads = window[0].reshape(key_rows, heads_here, HD)
    value_heads = window[1].reshape(key_rows, heads_here, HD)
    block_count = class_map.shape[1]
    classes = token_classes(class_map.reshape(heads_here, block_count, -1), tok_rows, key_rows)
    scores = jnp.einsum(
        "thd,uhd->htu", query_heads, key_heads, preferred_element_type=jnp.float32
    ) * (1.0 / math.sqrt(HD))
    masked = jnp.where(classes == 2, scores, -jnp.inf)
    row_max = jnp.max(masked, axis=2, keepdims=True)
    probs = jnp.exp(masked - row_max)
    exact_total = jnp.sum(probs, axis=2, keepdims=True)
    apply_values = functools.partial(
        jnp.einsum, "htu,uhd->htd", preferred_element_type=jnp.float32
    )
    exact_out = apply_values(probs.astype(jnp.bfloat16), value_heads) / exact_total
    affinity = jnp.einsum(
        "thd,uhd->htu",
        feature_map(query_heads),
        feature_map(key_heads),
        preferred_element_type=jnp.float32,
    )
    affinity = jnp.where(classes == 1, affinity, 0.0)
    linear_total = jnp.maximum(jnp.sum(affinity, axis=2, keepdims=True), 1.0)
    linear_out = apply_values(affinity.astype(jnp.bfloat16), value_heads) / linear_total
    attended = (
        (exact_out + linear_out)
        .transpose(1, 0, 2)
        .reshape(tok_rows, heads_here * HD)
        .astype(jnp.bfloat16)
    )
    partial_rows = lax.dot_general(
        attended,
        lax.all_gather(out_weight, "seq", axis=0, tiled=True),
        (((1,), (1,)), ((), ())),
        preferred_element_type=jnp.float32,
    )
    return lax.psum_scatter(
        partial_rows.astype(jnp.bfloat16), "head", scatter_dimension=0, tiled=True
    )


def moves(target):
    pairs = []
    for z in range(LINE):
        for j in range(PLANE):
            to = target(z, j)
            if to is not None:
                pairs.append((z * PLANE + j, to[0] * PLANE + to[1]))
    return pairs


PLANES = [[z * PLANE + j for j in range(PLANE)] for z in range(LINE)]
PLANE_SWAP = [moves(lambda z, j, turn=turn: (z, j ^ turn)) for turn in range(PLANE)]
NEXT_PLANE = moves(lambda z, j: ((z + 1) % LINE, j))
SWAP_PAIR = moves(lambda z, j: (z ^ 1, j))
SWAP_MID = moves(lambda z, j: (3 - z, j) if z in (1, 2) else None)
TO_ENDS = moves(lambda z, j: ({1: 0, 2: 3}[z], j) if z in (1, 2) else None)

CONTRACT_LAST = (((1,), (1,)), ((), ()))
CONTRACT_ROWS = (((1,), (0,)), ((), ()))
CONTRACT_FIRST = (((0,), (0,)), ((), ()))
SMEM = pl.BlockSpec(memory_space=pltpu.SMEM)
VMEM = pl.BlockSpec(memory_space=pltpu.VMEM)


def send(value, pairs):
    return lax.ppermute(value, "seq", pairs)


def exchange(value):
    return lax.all_to_all(value, "seq", 0, 0, tiled=True, axis_index_groups=PLANES)


def after(value, *others):
    return lax.optimization_barrier((value,) + others)[0]


def dot(left, right, dims):
    return lax.dot_general(left, right, dims, preferred_element_type=jnp.float32)


def pack_kernel(chunks, group, q_ref, k_ref, v_ref, *outs):
    first = 0
    for count, out in zip(chunks, outs):
        for owner in range(PLANE):
            for h in range(count):
                at = (owner * group + first + h) * HD
                for i, ref in enumerate((q_ref, k_ref, v_ref)):
                    out[owner, h, i] = ref[:, at : at + HD]
        first += count


def pack(chunks, group, queries, keys, values):
    tok = queries.shape[0]
    outs = [jax.ShapeDtypeStruct((PLANE, n, 3, tok, HD), jnp.bfloat16) for n in chunks]
    return pl.pallas_call(
        functools.partial(pack_kernel, chunks, group),
        out_shape=outs,
        in_specs=[VMEM] * 3,
        out_specs=[VMEM] * len(outs),
        compiler_params=pltpu.CompilerParams(vmem_limit_bytes=24 * 1024 * 1024),
        cost_estimate=pl.CostEstimate(
            flops=0, bytes_accessed=4 * 3 * queries.size, transcendentals=0
        ),
    )(queries, keys, values)


def attention_kernel(
    tok, count, own, last, last2, bias_ref, lin_ref, out_ref, q_all, k_all, v_all, s_all
):
    blocks = tok // BLOCK
    window = CYCLE * tok
    skipped = 2 * PLANE + 1 - CYCLE
    scale = math.log2(math.e) / math.sqrt(HD)
    v_all[:, HD:] = jnp.ones((v_all.shape[0], HD), jnp.bfloat16)

    def one_head(h, carry):
        def fill(get, places, first):
            def body(i, inner):
                k, v = get(i)
                at = pl.multiple_of((first + i) * tok, tok)
                k_all[pl.ds(at, tok), :] = k
                v_all[pl.ds(at, tok), :HD] = v
                f = feature_map(k)
                counted = jnp.concatenate([v, jnp.ones_like(v)], axis=1)
                for b in range(blocks):
                    block = slice(b * BLOCK, (b + 1) * BLOCK)
                    s_all[pl.ds(at + b * BLOCK, BLOCK), :] = dot(
                        f[block], counted[block], CONTRACT_FIRST
                    ).astype(jnp.bfloat16)
                return inner

            lax.fori_loop(0, places, body, 0)

        fill(lambda i: (last2[i, h, 0], last2[i, h, 1]), PLANE - skipped, 0)
        fill(lambda i: (last[i, h, 0], last[i, h, 1]), PLANE, PLANE - skipped)
        fill(lambda i: (own[i, h, 1], own[i, h, 2]), PLANE, 2 * PLANE - skipped)

        def one_shard(i, inner):
            rows = pl.ds(pl.multiple_of(i * tok, tok), window)
            q = own[i, h, 0]
            scores = dot(q, k_all[rows, :], CONTRACT_LAST)
            scores = scores.reshape(blocks, BLOCK, window) * scale + bias_ref[h, i][:, None, :]
            scores = scores.reshape(tok, window)
            probs = jnp.exp2(scores - jnp.max(scores, axis=1, keepdims=True))
            exact = dot(probs.astype(jnp.bfloat16), v_all[rows, :], CONTRACT_ROWS)
            f = jnp.concatenate([feature_map(q)] * (window // BLOCK), axis=1)
            f = (f.reshape(blocks, BLOCK, window) * lin_ref[h, i][:, None, :]).reshape(tok, window)
            linear = dot(f, s_all[rows, :], CONTRACT_ROWS)
            out_ref[i, h] = (
                exact[:, :HD] / exact[:, HD:] + linear[:, :HD] / jnp.maximum(linear[:, HD:], 1.0)
            ).astype(jnp.bfloat16)
            return inner

        lax.fori_loop(0, PLANE, one_shard, 0)
        return carry

    lax.fori_loop(0, count, one_head, 0)


def attention(own, last, last2, bias, lin):
    _, count, _, tok, _ = own.shape
    rows = (2 * PLANE + last2.shape[0]) * tok
    pairs = count * tok * PLANE * CYCLE * tok
    return pl.pallas_call(
        functools.partial(attention_kernel, tok, count),
        out_shape=jax.ShapeDtypeStruct((PLANE, count, tok, HD), jnp.bfloat16),
        in_specs=[VMEM] * 5,
        out_specs=VMEM,
        scratch_shapes=[
            pltpu.VMEM((16, HD), jnp.bfloat16),
            pltpu.VMEM((rows, HD), jnp.bfloat16),
            pltpu.VMEM((rows, 2 * HD), jnp.bfloat16),
            pltpu.VMEM((rows, 2 * HD), jnp.bfloat16),
        ],
        compiler_params=pltpu.CompilerParams(vmem_limit_bytes=48 * 1024 * 1024),
        cost_estimate=pl.CostEstimate(
            flops=8 * pairs * HD, bytes_accessed=8 * count * rows * HD, transcendentals=pairs
        ),
    )(own, last, last2, bias, lin)


def project_kernel(tok, group, spans, summed, place, *refs):
    j, core = place[1], place[2]
    sources = refs[: PLANE * len(spans)]
    refs = refs[PLANE * len(spans) :]
    pieces = []
    for two in summed:
        pieces.append(refs[: 1 + two])
        refs = refs[1 + two :]
    mine, theirs, left, weight = refs
    for g, (first, count) in enumerate(spans):
        for turn in range(PLANE):
            owner = jnp.bitwise_xor(j, turn)
            for h in range(count):
                lanes = pl.ds(pl.multiple_of((owner * group + first + h) * HD, HD), HD)
                for i in range(PLANE):
                    left[i * tok : (i + 1) * tok, lanes] = sources[PLANE * g + turn][i, h]

    for p, piece in enumerate(pieces):
        if len(piece) == 2:
            weight[...] = piece[0][...] + piece[1][...]
            source = weight
        else:
            source = piece[0]

        def one_shard(i, carry, p=p, source=source):
            rows = pl.ds(pl.multiple_of(i * tok, tok), tok)
            product = dot(left[rows, :], source[...], CONTRACT_LAST).astype(jnp.bfloat16)
            low, high = product[: tok // 2], product[tok // 2 :]
            mine[i, p] = jnp.where(core == 0, low, high)
            theirs[i, p] = jnp.where(core == 0, high, low)
            return carry

        lax.fori_loop(0, PLANE, one_shard, 0)


def project(place, group, spans, gathered, pieces):
    tok = gathered[0].shape[2]
    rows, depth = pieces[0][0].shape
    operands = [*gathered] + [a for piece in pieces for a in piece]
    shape = jax.ShapeDtypeStruct((PLANE, len(pieces), tok // 2, rows), jnp.bfloat16)
    return pl.pallas_call(
        functools.partial(project_kernel, tok, group, spans, tuple(len(p) - 1 for p in pieces)),
        out_shape=[shape] * 2,
        in_specs=[SMEM] + [VMEM] * len(operands),
        out_specs=[VMEM] * 2,
        scratch_shapes=[
            pltpu.VMEM((PLANE * tok, depth), jnp.bfloat16),
            pltpu.VMEM((rows, depth), jnp.bfloat16),
        ],
        compiler_params=pltpu.CompilerParams(vmem_limit_bytes=48 * 1024 * 1024),
        cost_estimate=pl.CostEstimate(
            flops=2 * PLANE * tok * rows * len(pieces) * depth,
            bytes_accessed=2 * depth * (PLANE * tok + len(pieces) * rows),
            transcendentals=0,
        ),
    )(place, *operands)


def two_level_plan(queries, keys, values, class_map, out_weight):
    tok = queries.shape[0]
    heads = queries.shape[1] // HD
    group = heads // PLANE
    chunks = CHUNKS if sum(CHUNKS) == group else (1,) * group
    steps = len(chunks)
    firsts = [sum(chunks[:t]) for t in range(steps)]
    spans = tuple(zip(firsts, chunks))
    here = lax.axis_index("seq")
    core = lax.axis_index("head")
    z, j = here // PLANE, here % PLANE
    place = jnp.stack([z, j, core]).astype(jnp.int32)
    skipped = 2 * PLANE + 1 - CYCLE

    packed = pack(chunks, group, queries, keys, values)

    weight_pair = send(after(out_weight, packed[0]), SWAP_PAIR)
    weight_mid = [send(after(out_weight, packed[0]), SWAP_MID), None]

    own, last, last2 = [], [], []
    for t in range(steps):
        message = packed[t] if t == 0 else after(packed[t], own[t - 1])
        own.append(exchange(message))
        if t == 1:
            weight_mid[1] = send(after(weight_pair, last[0]), SWAP_MID)
        current = own[t][:, :, 1:]
        if t:
            current = after(current, last[t - 1])
        last.append(send(current, NEXT_PLANE))
        last2.append(send(last[t][skipped:], NEXT_PLANE))
    weight_end = [send(after(weight_mid[0], last[-1]), TO_ENDS)]
    weight_end.append(send(after(weight_mid[1], weight_end[0]), TO_ENDS))

    parts = class_map.reshape((PLANE, group) + class_map.shape[1:])
    class_parts = []
    for turn in range(PLANE):
        part = lax.dynamic_index_in_dim(parts, jnp.bitwise_xor(j, turn), 0, keepdims=False)
        class_parts.append(send(part, PLANE_SWAP[turn]) if turn else part)
    class_parts = [
        jnp.where(j % 2 == 1, class_parts[i ^ 1], class_parts[i]) for i in range(PLANE)
    ]
    class_parts = [jnp.where(j >= 2, class_parts[i ^ 2], class_parts[i]) for i in range(PLANE)]
    classes = jnp.stack(class_parts, axis=1)[:, :, :, ::-1, :]
    classes = classes.reshape(classes.shape[:3] + (-1, 1))
    wide = jnp.broadcast_to(classes, classes.shape[:4] + (BLOCK,)).reshape(classes.shape[:3] + (-1,))
    bias = jnp.where(wide == 2, 0.0, MASKED).astype(jnp.float32)
    lin = jnp.where(wide == 1, 1.0, 0.0).astype(jnp.bfloat16)

    gathered = []
    for t in range(steps):
        some = slice(firsts[t], firsts[t] + chunks[t])
        att = attention(own[t], last[t], last2[t], bias[some], lin[some])
        gathered += [att] + [send(att, PLANE_SWAP[turn]) for turn in range(1, PLANE)]

    far = jnp.where(z < 2, 2, 1)
    plans = [
        (
            [(out_weight,), (weight_pair,), (weight_mid[0], weight_end[0])],
            [z, jnp.bitwise_xor(z, 1), far],
        ),
        ([(weight_mid[1], weight_end[1])], [jnp.bitwise_xor(far, 1)]),
    ]
    rows = out_weight.shape[0]
    out = jnp.zeros((tok // 2, LINE * PLANE * rows), jnp.bfloat16)
    before = None
    for pieces, lines in plans:
        if before is not None:
            pieces = [tuple(after(a, before) for a in piece) for piece in pieces]
        mine, theirs = project(place, group, spans, gathered, pieces)
        before = mine
        other = lax.ppermute(theirs, "head", [(0, 1), (1, 0)])
        both = (mine.astype(jnp.float32) + other.astype(jnp.float32)).astype(jnp.bfloat16)
        arrived = exchange(both)
        wide = jnp.concatenate([arrived[i] for i in range(PLANE)], axis=2)
        for p, line in enumerate(lines):
            out = lax.dynamic_update_slice_in_dim(out, wide[p], line * PLANE * rows, 1)
    return out


def solution(mesh):
    placed = (
        P("seq", "head"),
        P("seq", "head"),
        P("seq", "head"),
        P("head", "seq", None, None),
        P("seq", "head"),
    )

    def local(queries, *rest):
        heads_here = queries.shape[1] // HD
        two_level = (
            mesh.shape["seq"] == LINE * PLANE
            and mesh.shape["head"] == 2
            and heads_here % LINE == 0
        )
        return (two_level_plan if two_level else ring_plan)(queries, *rest)

    return jax.shard_map(
        local, mesh=mesh, in_specs=placed, out_specs=P(("seq", "head"), None), check_vma=False
    )
```

```python
import functools
import math

import jax
import jax.numpy as jnp
from jax import lax
from jax.experimental import pallas as pl
from jax.experimental.pallas import tpu as pltpu
from jax.sharding import PartitionSpec as P

HD = 128
CYCLE = 8
BLOCK = 128
LINE = 4
PLANE = 4
MASKED = -1e30
HEAVY = pl.CostEstimate(flops=10**10, bytes_accessed=2**24, transcendentals=0)
LIGHT = pl.CostEstimate(flops=1, bytes_accessed=1, transcendentals=0)


def feature_map(numbers):
    x = numbers.astype(jnp.float32)
    return jnp.where(x > 0, x + 1.0, jnp.exp(jnp.minimum(x, 0.0))).astype(jnp.bfloat16)


def passed_along(value, axis, steps):
    count = lax.axis_size(axis)
    pairs = [(source, (source + steps) % count) for source in range(count)]
    return lax.ppermute(value, axis, pairs)


def token_classes(block_row, tok_rows, key_rows):
    heads_here, query_blocks, key_blocks = block_row.shape
    query_width = tok_rows // query_blocks
    key_width = key_rows // key_blocks
    widened = jnp.broadcast_to(
        block_row[:, :, None, :, None],
        (heads_here, query_blocks, query_width, key_blocks, key_width),
    )
    return widened.reshape(heads_here, tok_rows, key_rows)


def ring_plan(queries, keys, values, class_map, out_weight):
    tok_rows = queries.shape[0]
    heads_here = queries.shape[1] // HD
    current = jnp.stack([keys, values])
    arrivals = [current]
    for _ in range(1, CYCLE):
        current = passed_along(current, "seq", 1)
        arrivals.append(current)
    window = jnp.concatenate(arrivals, axis=1)
    key_rows = window.shape[1]
    query_heads = queries.reshape(tok_rows, heads_here, HD)
    key_heads = window[0].reshape(key_rows, heads_here, HD)
    value_heads = window[1].reshape(key_rows, heads_here, HD)
    block_count = class_map.shape[1]
    classes = token_classes(class_map.reshape(heads_here, block_count, -1), tok_rows, key_rows)
    scores = jnp.einsum(
        "thd,uhd->htu", query_heads, key_heads, preferred_element_type=jnp.float32
    ) * (1.0 / math.sqrt(HD))
    masked = jnp.where(classes == 2, scores, -jnp.inf)
    row_max = jnp.max(masked, axis=2, keepdims=True)
    probs = jnp.exp(masked - row_max)
    exact_total = jnp.sum(probs, axis=2, keepdims=True)
    apply_values = functools.partial(
        jnp.einsum, "htu,uhd->htd", preferred_element_type=jnp.float32
    )
    exact_out = apply_values(probs.astype(jnp.bfloat16), value_heads) / exact_total
    affinity = jnp.einsum(
        "thd,uhd->htu",
        feature_map(query_heads),
        feature_map(key_heads),
        preferred_element_type=jnp.float32,
    )
    affinity = jnp.where(classes == 1, affinity, 0.0)
    linear_total = jnp.maximum(jnp.sum(affinity, axis=2, keepdims=True), 1.0)
    linear_out = apply_values(affinity.astype(jnp.bfloat16), value_heads) / linear_total
    attended = (
        (exact_out + linear_out)
        .transpose(1, 0, 2)
        .reshape(tok_rows, heads_here * HD)
        .astype(jnp.bfloat16)
    )
    partial_rows = lax.dot_general(
        attended,
        lax.all_gather(out_weight, "seq", axis=0, tiled=True),
        (((1,), (1,)), ((), ())),
        preferred_element_type=jnp.float32,
    )
    return lax.psum_scatter(
        partial_rows.astype(jnp.bfloat16), "head", scatter_dimension=0, tiled=True
    )


def moves(target):
    pairs = []
    for z in range(LINE):
        for j in range(PLANE):
            to = target(z, j)
            if to is not None:
                pairs.append((z * PLANE + j, to[0] * PLANE + to[1]))
    return pairs


PLANES = [[z * PLANE + j for j in range(PLANE)] for z in range(LINE)]
PLANE_SWAP = [moves(lambda z, j, turn=turn: (z, j ^ turn)) for turn in range(PLANE)]
NEXT_PLANE = moves(lambda z, j: ((z + 1) % LINE, j))
SWAP_PAIR = moves(lambda z, j: (z ^ 1, j))
SWAP_MID = moves(lambda z, j: (3 - z, j) if z in (1, 2) else None)
TO_ENDS = moves(lambda z, j: ({1: 0, 2: 3}[z], j) if z in (1, 2) else None)

CONTRACT_LAST = (((1,), (1,)), ((), ()))
CONTRACT_ROWS = (((1,), (0,)), ((), ()))
CONTRACT_FIRST = (((0,), (0,)), ((), ()))
SMEM = pl.BlockSpec(memory_space=pltpu.SMEM)
VMEM = pl.BlockSpec(memory_space=pltpu.VMEM)


def send(value, pairs):
    return lax.ppermute(value, "seq", pairs)


def exchange(value):
    return lax.all_to_all(value, "seq", 0, 0, tiled=True, axis_index_groups=PLANES)


def after(value, *others):
    return lax.optimization_barrier((value,) + others)[0]


def dot(left, right, dims):
    return lax.dot_general(left, right, dims, preferred_element_type=jnp.float32)


def together(*values):
    return lax.optimization_barrier(values)


def pack_kernel(group, count, *refs):
    out = refs[count]
    for owner in range(PLANE):
        for h in range(group):
            at = (owner * group + h) * HD
            for i in range(count):
                out[owner, h, i] = refs[i][:, at : at + HD]


def pack(group, *arrays):
    tok = arrays[0].shape[0]
    shape = (PLANE, group, len(arrays), tok, HD)
    return pl.pallas_call(
        functools.partial(pack_kernel, group, len(arrays)),
        out_shape=jax.ShapeDtypeStruct(shape, jnp.bfloat16),
        in_specs=[VMEM] * len(arrays),
        out_specs=VMEM,
        compiler_params=pltpu.CompilerParams(vmem_limit_bytes=24 * 1024 * 1024),
        cost_estimate=pl.CostEstimate(
            flops=0, bytes_accessed=4 * len(arrays) * arrays[0].size, transcendentals=0
        ),
    )(*arrays)


def attention_kernel(tok, q_ref, own, last, last2, bias_ref, lin_ref, out_ref, k_all, v_all, s_all):
    blocks = tok // BLOCK
    window = CYCLE * tok
    skipped = 2 * PLANE + 1 - CYCLE
    scale = math.log2(math.e) / math.sqrt(HD)

    @pl.when(pl.program_id(0) == 0)
    def _():
        v_all[:, HD:] = jnp.ones((v_all.shape[0], HD), jnp.bfloat16)

    def fill(ref, places, first):
        def body(i, carry):
            k, v = ref[i, 0, 0], ref[i, 0, 1]
            at = pl.multiple_of((first + i) * tok, tok)
            k_all[pl.ds(at, tok), :] = k
            v_all[pl.ds(at, tok), :HD] = v
            f = feature_map(k)
            counted = jnp.concatenate([v, jnp.ones_like(v)], axis=1)
            for b in range(blocks):
                block = slice(b * BLOCK, (b + 1) * BLOCK)
                s_all[pl.ds(at + b * BLOCK, BLOCK), :] = dot(
                    f[block], counted[block], CONTRACT_FIRST
                ).astype(jnp.bfloat16)
            return carry

        lax.fori_loop(0, places, body, 0)

    fill(last2, PLANE - skipped, 0)
    fill(last, PLANE, PLANE - skipped)
    fill(own, PLANE, 2 * PLANE - skipped)

    def one_shard(i, carry):
        rows = pl.ds(pl.multiple_of(i * tok, tok), window)
        q = q_ref[i, 0, 0]
        scores = dot(q, k_all[rows, :], CONTRACT_LAST)
        scores = scores.reshape(blocks, BLOCK, window) * scale + bias_ref[0, i][:, None, :]
        scores = scores.reshape(tok, window)
        probs = jnp.exp2(scores - jnp.max(scores, axis=1, keepdims=True))
        exact = dot(probs.astype(jnp.bfloat16), v_all[rows, :], CONTRACT_ROWS)
        f = jnp.concatenate([feature_map(q)] * (window // BLOCK), axis=1)
        f = (f.reshape(blocks, BLOCK, window) * lin_ref[0, i][:, None, :]).reshape(tok, window)
        linear = dot(f, s_all[rows, :], CONTRACT_ROWS)
        out_ref[i, 0] = (
            exact[:, :HD] / exact[:, HD:] + linear[:, :HD] / jnp.maximum(linear[:, HD:], 1.0)
        ).astype(jnp.bfloat16)
        return carry

    lax.fori_loop(0, PLANE, one_shard, 0)


def attention(first, count, q, own, last, last2, bias, lin):
    tok = q.shape[3]
    rows = (2 * PLANE + last2.shape[0]) * tok
    pairs = count * tok * PLANE * CYCLE * tok

    def heads(array, start):
        shape = array.shape[:1] + (1,) + array.shape[2:]
        zeros = (0,) * (array.ndim - 2)
        return pl.BlockSpec(shape, lambda h: (0, start + h) + zeros)

    def masks(array):
        return pl.BlockSpec((1,) + array.shape[1:], lambda h: (first + h, 0, 0, 0))

    return pl.pallas_call(
        functools.partial(attention_kernel, tok),
        grid=(count,),
        out_shape=jax.ShapeDtypeStruct((PLANE, count, tok, HD), jnp.bfloat16),
        in_specs=[heads(q, first), heads(own, first), heads(last, first), heads(last2, 0)]
        + [masks(bias), masks(lin)],
        out_specs=pl.BlockSpec((PLANE, 1, tok, HD), lambda h: (0, h, 0, 0)),
        scratch_shapes=[
            pltpu.VMEM((rows, HD), jnp.bfloat16),
            pltpu.VMEM((rows, 2 * HD), jnp.bfloat16),
            pltpu.VMEM((rows, 2 * HD), jnp.bfloat16),
        ],
        compiler_params=pltpu.CompilerParams(vmem_limit_bytes=48 * 1024 * 1024),
        cost_estimate=pl.CostEstimate(
            flops=8 * pairs * HD, bytes_accessed=8 * count * rows * HD, transcendentals=pairs
        ),
    )(q, own, last, last2, bias, lin)


def project_kernel(tok, group, spans, summed, begun, ends, place, *refs):
    j, core = place[1], place[2]
    sources = refs[: PLANE * len(spans)]
    refs = refs[PLANE * len(spans) :]
    pieces = []
    for two in summed:
        pieces.append(refs[: 1 + two])
        refs = refs[1 + two :]
    so_far = refs[0] if begun else None
    *outs, left, weight = refs[1 if begun else 0 :]
    blocks = []
    base = 0
    for g, (first, count) in enumerate(spans):
        width = count * HD
        for turn in range(PLANE):
            owner = jnp.bitwise_xor(j, turn)
            for h in range(count):
                lanes = pl.ds(pl.multiple_of(base + owner * width + h * HD, HD), HD)
                for i in range(PLANE):
                    left[i * tok : (i + 1) * tok, lanes] = sources[PLANE * g + turn][i, h]
        for owner in range(PLANE):
            there = (owner * group + first) * HD
            blocks.append((base + owner * width, there, width))
        base += PLANE * width

    for p, piece in enumerate(pieces):
        if len(piece) == 2:
            weight[...] = piece[0][...] + piece[1][...]
            source = weight
        else:
            source = piece[0]

        def one_shard(i, carry, p=p, source=source):
            rows = pl.ds(pl.multiple_of(i * tok, tok), tok)
            product = so_far[i, p] if begun else None
            for here, there, width in blocks:
                term = dot(
                    source[:, there : there + width], left[rows, here : here + width], CONTRACT_LAST
                )
                product = term if product is None else product + term
            if not ends:
                outs[0][i, p] = product
                return carry
            product = product.astype(jnp.bfloat16)
            low, high = product[:, : tok // 2], product[:, tok // 2 :]
            outs[0][i, p] = jnp.where(core == 0, low, high)
            outs[1][i, p] = jnp.where(core == 0, high, low)
            return carry

        lax.fori_loop(0, PLANE, one_shard, 0)


def project(place, group, spans, gathered, pieces, so_far=None, ends=True, cost=LIGHT):
    tok = gathered[0].shape[2]
    rows, depth = pieces[0][0].shape
    operands = [*gathered] + [a for piece in pieces for a in piece]
    if so_far is not None:
        operands.append(so_far)
    if ends:
        outs = [jax.ShapeDtypeStruct((PLANE, len(pieces), rows, tok // 2), jnp.bfloat16)] * 2
    else:
        outs = [jax.ShapeDtypeStruct((PLANE, len(pieces), rows, tok), jnp.float32)]
    some = sum(count for _, count in spans) * PLANE * HD
    return pl.pallas_call(
        functools.partial(
            project_kernel,
            tok,
            group,
            spans,
            tuple(len(p) - 1 for p in pieces),
            so_far is not None,
            ends,
        ),
        out_shape=outs,
        in_specs=[SMEM] + [VMEM] * len(operands),
        out_specs=[VMEM] * len(outs),
        scratch_shapes=[
            pltpu.VMEM((PLANE * tok, some), jnp.bfloat16),
            pltpu.VMEM((rows, depth), jnp.bfloat16),
        ],
        compiler_params=pltpu.CompilerParams(vmem_limit_bytes=48 * 1024 * 1024),
        cost_estimate=cost,
    )(place, *operands)


def two_level_plan(queries, keys, values, class_map, out_weight):
    tok = queries.shape[0]
    heads = queries.shape[1] // HD
    group = heads // PLANE
    early = max(1, 3 * group // 5)
    spans = ((0, early), (early, group - early))
    here = lax.axis_index("seq")
    core = lax.axis_index("head")
    z, j = here // PLANE, here % PLANE
    place = jnp.stack([z, j, core]).astype(jnp.int32)
    skipped = 2 * PLANE + 1 - CYCLE

    packed = pack(group, keys, values)
    weight_pair = send(out_weight, SWAP_PAIR)
    weight_mid = send(out_weight, SWAP_MID)
    own, queries, weight_pair, weight_mid = together(
        exchange(packed), queries, weight_pair, weight_mid
    )

    q = exchange(pack(group, queries))
    last = send(own, NEXT_PLANE)
    parts = after(class_map, own).reshape((PLANE, group) + class_map.shape[1:])
    class_parts = []
    for turn in range(PLANE):
        part = lax.dynamic_index_in_dim(parts, jnp.bitwise_xor(j, turn), 0, keepdims=False)
        class_parts.append(send(part, PLANE_SWAP[turn]) if turn else part)
    class_parts = [
        jnp.where(j % 2 == 1, class_parts[i ^ 1], class_parts[i]) for i in range(PLANE)
    ]
    class_parts = [jnp.where(j >= 2, class_parts[i ^ 2], class_parts[i]) for i in range(PLANE)]
    classes = jnp.stack(class_parts, axis=1)[:, :, :, ::-1, :]
    classes = classes.reshape(classes.shape[:3] + (-1, 1))
    wide = jnp.broadcast_to(classes, classes.shape[:4] + (BLOCK,)).reshape(classes.shape[:3] + (-1,))
    bias = jnp.where(wide == 2, 0.0, MASKED).astype(jnp.float32)
    lin = jnp.where(wide == 1, 1.0, 0.0).astype(jnp.bfloat16)

    q, own, last, bias, lin, weight_pair, weight_mid = together(
        q, own, last, bias, lin, weight_pair, weight_mid
    )

    behind = last[skipped:]
    last2 = send(behind[:, :early], NEXT_PLANE)
    late2 = send(after(behind[:, early:], last2), NEXT_PLANE)
    att = attention(0, early, q, own, last, last2, bias, lin)
    q, own, last, late2, att, bias, lin, weight_pair, weight_mid = together(
        q, own, last, late2, att, bias, lin, weight_pair, weight_mid
    )

    weight_end = send(weight_mid, TO_ENDS)
    weight_mid2 = send(weight_pair, SWAP_MID)
    gathered = [att] + [send(att, PLANE_SWAP[turn]) for turn in range(1, PLANE)]
    late = attention(early, group - early, q, own, last, late2, bias, lin)
    late, weight_pair, weight_mid, weight_end, weight_mid2, *gathered = together(
        late, weight_pair, weight_mid, weight_end, weight_mid2, *gathered
    )

    weight_end2 = send(weight_mid2, TO_ENDS)
    gathered += [late] + [send(late, PLANE_SWAP[turn]) for turn in range(1, PLANE)]
    far = jnp.where(z < 2, 2, 1)
    rows = out_weight.shape[0]
    out = jnp.zeros((tok // 2, LINE * PLANE * rows), jnp.bfloat16)

    def summed(mine, theirs):
        other = lax.ppermute(theirs, "head", [(0, 1), (1, 0)])
        return (mine.astype(jnp.float32) + other.astype(jnp.float32)).astype(jnp.bfloat16)

    def place_rows(out, arrived, lines):
        for p, line in enumerate(lines):
            wide = arrived[:, p].reshape(PLANE * rows, tok // 2).T
            out = lax.dynamic_update_slice_in_dim(out, wide, line * PLANE * rows, 1)
        return out

    pieces = [(out_weight,), (weight_pair,), (weight_mid, weight_end)]
    (so_far,) = project(place, group, spans[:1], gathered[:PLANE], pieces, ends=False)
    mine, theirs = project(place, group, spans[1:], gathered[PLANE:], pieces, so_far)
    mine, theirs, weight_mid2, weight_end2, *gathered = together(
        mine, theirs, weight_mid2, weight_end2, *gathered
    )

    both, weight_mid2, weight_end2 = together(summed(mine, theirs), weight_mid2, weight_end2)
    arrived = exchange(both)
    mine2, theirs2 = project(
        place, group, spans, gathered, [(weight_mid2, weight_end2)], cost=HEAVY
    )
    both2, arrived = together(summed(mine2, theirs2), arrived)
    turns = [
        lax.dynamic_index_in_dim(both2, jnp.bitwise_xor(j, turn), 0, keepdims=False)
        for turn in range(PLANE)
    ]
    turns = turns[:1] + [send(turns[turn], PLANE_SWAP[turn]) for turn in range(1, PLANE)]
    turns = [jnp.where(j % 2 == 1, turns[i ^ 1], turns[i]) for i in range(PLANE)]
    turns = [jnp.where(j >= 2, turns[i ^ 2], turns[i]) for i in range(PLANE)]
    out = place_rows(out, arrived, [z, jnp.bitwise_xor(z, 1), far])
    return place_rows(out, jnp.stack(turns), [jnp.bitwise_xor(far, 1)])


def solution(mesh):
    placed = (
        P("seq", "head"),
        P("seq", "head"),
        P("seq", "head"),
        P("head", "seq", None, None),
        P("seq", "head"),
    )

    def local(queries, *rest):
        heads_here = queries.shape[1] // HD
        two_level = (
            mesh.shape["seq"] == LINE * PLANE
            and mesh.shape["head"] == 2
            and heads_here % LINE == 0
        )
        return (two_level_plan if two_level else ring_plan)(queries, *rest)

    return jax.shard_map(
        local, mesh=mesh, in_specs=placed, out_specs=P(("seq", "head"), None), check_vma=False
    )
```

```python
import functools
import math

import jax
import jax.numpy as jnp
from jax import lax
from jax.experimental import pallas as pl
from jax.experimental.pallas import tpu as pltpu
from jax.sharding import PartitionSpec as P

HD = 128
CYCLE = 8
BLOCK = 128
LINE = 4
PLANE = 4
MASKED = -1e30
HEAVY = pl.CostEstimate(flops=10**10, bytes_accessed=2**24, transcendentals=0)
LIGHT = pl.CostEstimate(flops=1, bytes_accessed=1, transcendentals=0)


def feature_map(numbers):
    x = numbers.astype(jnp.float32)
    return jnp.where(x > 0, x + 1.0, jnp.exp(jnp.minimum(x, 0.0))).astype(jnp.bfloat16)


def passed_along(value, axis, steps):
    count = lax.axis_size(axis)
    pairs = [(source, (source + steps) % count) for source in range(count)]
    return lax.ppermute(value, axis, pairs)


def token_classes(block_row, tok_rows, key_rows):
    heads_here, query_blocks, key_blocks = block_row.shape
    query_width = tok_rows // query_blocks
    key_width = key_rows // key_blocks
    widened = jnp.broadcast_to(
        block_row[:, :, None, :, None],
        (heads_here, query_blocks, query_width, key_blocks, key_width),
    )
    return widened.reshape(heads_here, tok_rows, key_rows)


def ring_plan(queries, keys, values, class_map, out_weight):
    tok_rows = queries.shape[0]
    heads_here = queries.shape[1] // HD
    current = jnp.stack([keys, values])
    arrivals = [current]
    for _ in range(1, CYCLE):
        current = passed_along(current, "seq", 1)
        arrivals.append(current)
    window = jnp.concatenate(arrivals, axis=1)
    key_rows = window.shape[1]
    query_heads = queries.reshape(tok_rows, heads_here, HD)
    key_heads = window[0].reshape(key_rows, heads_here, HD)
    value_heads = window[1].reshape(key_rows, heads_here, HD)
    block_count = class_map.shape[1]
    classes = token_classes(class_map.reshape(heads_here, block_count, -1), tok_rows, key_rows)
    scores = jnp.einsum(
        "thd,uhd->htu", query_heads, key_heads, preferred_element_type=jnp.float32
    ) * (1.0 / math.sqrt(HD))
    masked = jnp.where(classes == 2, scores, -jnp.inf)
    row_max = jnp.max(masked, axis=2, keepdims=True)
    probs = jnp.exp(masked - row_max)
    exact_total = jnp.sum(probs, axis=2, keepdims=True)
    apply_values = functools.partial(
        jnp.einsum, "htu,uhd->htd", preferred_element_type=jnp.float32
    )
    exact_out = apply_values(probs.astype(jnp.bfloat16), value_heads) / exact_total
    affinity = jnp.einsum(
        "thd,uhd->htu",
        feature_map(query_heads),
        feature_map(key_heads),
        preferred_element_type=jnp.float32,
    )
    affinity = jnp.where(classes == 1, affinity, 0.0)
    linear_total = jnp.maximum(jnp.sum(affinity, axis=2, keepdims=True), 1.0)
    linear_out = apply_values(affinity.astype(jnp.bfloat16), value_heads) / linear_total
    attended = (
        (exact_out + linear_out)
        .transpose(1, 0, 2)
        .reshape(tok_rows, heads_here * HD)
        .astype(jnp.bfloat16)
    )
    partial_rows = lax.dot_general(
        attended,
        lax.all_gather(out_weight, "seq", axis=0, tiled=True),
        (((1,), (1,)), ((), ())),
        preferred_element_type=jnp.float32,
    )
    return lax.psum_scatter(
        partial_rows.astype(jnp.bfloat16), "head", scatter_dimension=0, tiled=True
    )


def moves(target):
    pairs = []
    for z in range(LINE):
        for j in range(PLANE):
            to = target(z, j)
            if to is not None:
                pairs.append((z * PLANE + j, to[0] * PLANE + to[1]))
    return pairs


PLANES = [[z * PLANE + j for j in range(PLANE)] for z in range(LINE)]
PLANE_SWAP = [moves(lambda z, j, turn=turn: (z, j ^ turn)) for turn in range(PLANE)]
NEXT_PLANE = moves(lambda z, j: ((z + 1) % LINE, j))
SWAP_PAIR = moves(lambda z, j: (z ^ 1, j))
SWAP_MID = moves(lambda z, j: (3 - z, j) if z in (1, 2) else None)
TO_ENDS = moves(lambda z, j: ({1: 0, 2: 3}[z], j) if z in (1, 2) else None)

CONTRACT_LAST = (((1,), (1,)), ((), ()))
CONTRACT_ROWS = (((1,), (0,)), ((), ()))
CONTRACT_FIRST = (((0,), (0,)), ((), ()))
SMEM = pl.BlockSpec(memory_space=pltpu.SMEM)
VMEM = pl.BlockSpec(memory_space=pltpu.VMEM)


def send(value, pairs):
    return lax.ppermute(value, "seq", pairs)


def exchange(value):
    return lax.all_to_all(value, "seq", 0, 0, tiled=True, axis_index_groups=PLANES)


def after(value, *others):
    return lax.optimization_barrier((value,) + others)[0]


def dot(left, right, dims):
    return lax.dot_general(left, right, dims, preferred_element_type=jnp.float32)


def together(*values):
    return lax.optimization_barrier(values)


def pack_kernel(group, count, *refs):
    out = refs[count]
    for owner in range(PLANE):
        for h in range(group):
            at = (owner * group + h) * HD
            for i in range(count):
                out[owner, h, i] = refs[i][:, at : at + HD]


def pack(group, *arrays):
    tok = arrays[0].shape[0]
    shape = (PLANE, group, len(arrays), tok, HD)
    return pl.pallas_call(
        functools.partial(pack_kernel, group, len(arrays)),
        out_shape=jax.ShapeDtypeStruct(shape, jnp.bfloat16),
        in_specs=[VMEM] * len(arrays),
        out_specs=VMEM,
        compiler_params=pltpu.CompilerParams(vmem_limit_bytes=24 * 1024 * 1024),
        cost_estimate=pl.CostEstimate(
            flops=0, bytes_accessed=4 * len(arrays) * arrays[0].size, transcendentals=0
        ),
    )(*arrays)


def attention_kernel(tok, q_ref, own, last, last2, bias_ref, lin_ref, out_ref, k_all, v_all, s_all):
    blocks = tok // BLOCK
    window = CYCLE * tok
    skipped = 2 * PLANE + 1 - CYCLE
    scale = math.log2(math.e) / math.sqrt(HD)

    @pl.when(pl.program_id(0) == 0)
    def _():
        v_all[:, HD:] = jnp.ones((v_all.shape[0], HD), jnp.bfloat16)

    def fill(ref, places, first):
        def body(i, carry):
            k, v = ref[i, 0, 0], ref[i, 0, 1]
            at = pl.multiple_of((first + i) * tok, tok)
            k_all[pl.ds(at, tok), :] = k
            v_all[pl.ds(at, tok), :HD] = v
            f = feature_map(k)
            counted = jnp.concatenate([v, jnp.ones_like(v)], axis=1)
            for b in range(blocks):
                block = slice(b * BLOCK, (b + 1) * BLOCK)
                s_all[pl.ds(at + b * BLOCK, BLOCK), :] = dot(
                    f[block], counted[block], CONTRACT_FIRST
                ).astype(jnp.bfloat16)
            return carry

        lax.fori_loop(0, places, body, 0, unroll=True)

    fill(last2, PLANE - skipped, 0)
    fill(last, PLANE, PLANE - skipped)
    fill(own, PLANE, 2 * PLANE - skipped)

    def one_shard(i, carry):
        rows = pl.ds(pl.multiple_of(i * tok, tok), window)
        q = q_ref[i, 0, 0]
        scores = dot(q, k_all[rows, :], CONTRACT_LAST)
        scores = scores.reshape(blocks, BLOCK, window) * scale + bias_ref[0, i][:, None, :]
        scores = scores.reshape(tok, window)
        probs = jnp.exp2(scores - jnp.max(scores, axis=1, keepdims=True))
        exact = dot(probs.astype(jnp.bfloat16), v_all[rows, :], CONTRACT_ROWS)
        f = jnp.concatenate([feature_map(q)] * (window // BLOCK), axis=1)
        f = (f.reshape(blocks, BLOCK, window) * lin_ref[0, i][:, None, :]).reshape(tok, window)
        linear = dot(f, s_all[rows, :], CONTRACT_ROWS)
        out_ref[i, 0] = (
            exact[:, :HD] / exact[:, HD:] + linear[:, :HD] / jnp.maximum(linear[:, HD:], 1.0)
        ).astype(jnp.bfloat16)
        return carry

    lax.fori_loop(0, PLANE, one_shard, 0, unroll=2)


def attention(first, count, q, own, last, last2, bias, lin):
    tok = q.shape[3]
    rows = (2 * PLANE + last2.shape[0]) * tok
    pairs = count * tok * PLANE * CYCLE * tok

    def heads(array, start):
        shape = array.shape[:1] + (1,) + array.shape[2:]
        zeros = (0,) * (array.ndim - 2)
        return pl.BlockSpec(shape, lambda h: (0, start + h) + zeros)

    def masks(array):
        return pl.BlockSpec((1,) + array.shape[1:], lambda h: (first + h, 0, 0, 0))

    return pl.pallas_call(
        functools.partial(attention_kernel, tok),
        grid=(count,),
        out_shape=jax.ShapeDtypeStruct((PLANE, count, tok, HD), jnp.bfloat16),
        in_specs=[heads(q, first), heads(own, first), heads(last, first), heads(last2, 0)]
        + [masks(bias), masks(lin)],
        out_specs=pl.BlockSpec((PLANE, 1, tok, HD), lambda h: (0, h, 0, 0)),
        scratch_shapes=[
            pltpu.VMEM((rows, HD), jnp.bfloat16),
            pltpu.VMEM((rows, 2 * HD), jnp.bfloat16),
            pltpu.VMEM((rows, 2 * HD), jnp.bfloat16),
        ],
        compiler_params=pltpu.CompilerParams(vmem_limit_bytes=48 * 1024 * 1024),
        cost_estimate=pl.CostEstimate(
            flops=8 * pairs * HD, bytes_accessed=8 * count * rows * HD, transcendentals=pairs
        ),
    )(q, own, last, last2, bias, lin)


def project_kernel(tok, group, spans, summed, begun, ends, place, *refs):
    j, core = place[1], place[2]
    sources = refs[: PLANE * len(spans)]
    refs = refs[PLANE * len(spans) :]
    pieces = []
    for two in summed:
        pieces.append(refs[: 1 + two])
        refs = refs[1 + two :]
    so_far = refs[0] if begun else None
    *outs, left, weight = refs[1 if begun else 0 :]
    blocks = []
    base = 0
    for g, (first, count) in enumerate(spans):
        width = count * HD
        for turn in range(PLANE):
            owner = jnp.bitwise_xor(j, turn)
            for h in range(count):
                lanes = pl.ds(pl.multiple_of(base + owner * width + h * HD, HD), HD)
                for i in range(PLANE):
                    left[i * tok : (i + 1) * tok, lanes] = sources[PLANE * g + turn][i, h]
        for owner in range(PLANE):
            there = (owner * group + first) * HD
            blocks.append((base + owner * width, there, width))
        base += PLANE * width

    for p, piece in enumerate(pieces):
        if len(piece) == 2:
            weight[...] = piece[0][...] + piece[1][...]
            source = weight
        else:
            source = piece[0]

        def one_shard(i, carry, p=p, source=source):
            rows = pl.ds(pl.multiple_of(i * tok, tok), tok)
            product = so_far[i, p] if begun else None
            for here, there, width in blocks:
                term = dot(
                    source[:, there : there + width], left[rows, here : here + width], CONTRACT_LAST
                )
                product = term if product is None else product + term
            if not ends:
                outs[0][i, p] = product
                return carry
            product = product.astype(jnp.bfloat16)
            low, high = product[:, : tok // 2], product[:, tok // 2 :]
            outs[0][i, p] = jnp.where(core == 0, low, high)
            outs[1][i, p] = jnp.where(core == 0, high, low)
            return carry

        lax.fori_loop(0, PLANE, one_shard, 0)


def project(place, group, spans, gathered, pieces, so_far=None, ends=True, cost=LIGHT):
    tok = gathered[0].shape[2]
    rows, depth = pieces[0][0].shape
    operands = [*gathered] + [a for piece in pieces for a in piece]
    if so_far is not None:
        operands.append(so_far)
    if ends:
        outs = [jax.ShapeDtypeStruct((PLANE, len(pieces), rows, tok // 2), jnp.bfloat16)] * 2
    else:
        outs = [jax.ShapeDtypeStruct((PLANE, len(pieces), rows, tok), jnp.float32)]
    some = sum(count for _, count in spans) * PLANE * HD
    return pl.pallas_call(
        functools.partial(
            project_kernel,
            tok,
            group,
            spans,
            tuple(len(p) - 1 for p in pieces),
            so_far is not None,
            ends,
        ),
        out_shape=outs,
        in_specs=[SMEM] + [VMEM] * len(operands),
        out_specs=[VMEM] * len(outs),
        scratch_shapes=[
            pltpu.VMEM((PLANE * tok, some), jnp.bfloat16),
            pltpu.VMEM((rows, depth), jnp.bfloat16),
        ],
        compiler_params=pltpu.CompilerParams(vmem_limit_bytes=48 * 1024 * 1024),
        cost_estimate=cost,
    )(place, *operands)


def two_level_plan(queries, keys, values, class_map, out_weight):
    tok = queries.shape[0]
    heads = queries.shape[1] // HD
    group = heads // PLANE
    early = max(1, 3 * group // 5)
    spans = ((0, early), (early, group - early))
    here = lax.axis_index("seq")
    core = lax.axis_index("head")
    z, j = here // PLANE, here % PLANE
    place = jnp.stack([z, j, core]).astype(jnp.int32)
    skipped = 2 * PLANE + 1 - CYCLE

    packed = pack(group, keys, values)
    weight_pair = send(out_weight, SWAP_PAIR)
    weight_mid = send(out_weight, SWAP_MID)
    own, queries, weight_pair, weight_mid = together(
        exchange(packed), queries, weight_pair, weight_mid
    )

    q = exchange(pack(group, queries))
    last = send(own, NEXT_PLANE)
    parts = after(class_map, own).reshape((PLANE, group) + class_map.shape[1:])
    class_parts = []
    for turn in range(PLANE):
        part = lax.dynamic_index_in_dim(parts, jnp.bitwise_xor(j, turn), 0, keepdims=False)
        class_parts.append(send(part, PLANE_SWAP[turn]) if turn else part)
    class_parts = [
        jnp.where(j % 2 == 1, class_parts[i ^ 1], class_parts[i]) for i in range(PLANE)
    ]
    class_parts = [jnp.where(j >= 2, class_parts[i ^ 2], class_parts[i]) for i in range(PLANE)]
    classes = jnp.stack(class_parts, axis=1)[:, :, :, ::-1, :]
    classes = classes.reshape(classes.shape[:3] + (-1, 1))
    wide = jnp.broadcast_to(classes, classes.shape[:4] + (BLOCK,)).reshape(classes.shape[:3] + (-1,))
    bias = jnp.where(wide == 2, 0.0, MASKED).astype(jnp.float32)
    lin = jnp.where(wide == 1, 1.0, 0.0).astype(jnp.bfloat16)

    q, own, last, bias, lin, weight_pair, weight_mid = together(
        q, own, last, bias, lin, weight_pair, weight_mid
    )

    behind = last[skipped:]
    last2 = send(behind[:, :early], NEXT_PLANE)
    late2 = send(after(behind[:, early:], last2), NEXT_PLANE)
    att = attention(0, early, q, own, last, last2, bias, lin)
    q, own, last, late2, att, bias, lin, weight_pair, weight_mid = together(
        q, own, last, late2, att, bias, lin, weight_pair, weight_mid
    )

    weight_end = send(weight_mid, TO_ENDS)
    weight_mid2 = send(weight_pair, SWAP_MID)
    gathered = [att] + [send(att, PLANE_SWAP[turn]) for turn in range(1, PLANE)]
    late = attention(early, group - early, q, own, last, late2, bias, lin)
    late, weight_pair, weight_mid, weight_end, weight_mid2, *gathered = together(
        late, weight_pair, weight_mid, weight_end, weight_mid2, *gathered
    )

    weight_end2 = send(weight_mid2, TO_ENDS)
    gathered += [late] + [send(late, PLANE_SWAP[turn]) for turn in range(1, PLANE)]
    far = jnp.where(z < 2, 2, 1)
    rows = out_weight.shape[0]
    out = jnp.zeros((tok // 2, LINE * PLANE * rows), jnp.bfloat16)

    def summed(mine, theirs):
        other = lax.ppermute(theirs, "head", [(0, 1), (1, 0)])
        return (mine.astype(jnp.float32) + other.astype(jnp.float32)).astype(jnp.bfloat16)

    def place_rows(out, arrived, lines):
        for p, line in enumerate(lines):
            wide = arrived[:, p].reshape(PLANE * rows, tok // 2).T
            out = lax.dynamic_update_slice_in_dim(out, wide, line * PLANE * rows, 1)
        return out

    pieces = [(out_weight,), (weight_pair,), (weight_mid, weight_end)]
    (so_far,) = project(place, group, spans[:1], gathered[:PLANE], pieces, ends=False)
    mine, theirs = project(place, group, spans[1:], gathered[PLANE:], pieces, so_far)
    mine, theirs, weight_mid2, weight_end2, *gathered = together(
        mine, theirs, weight_mid2, weight_end2, *gathered
    )

    both, weight_mid2, weight_end2 = together(summed(mine, theirs), weight_mid2, weight_end2)
    arrived = exchange(both)
    mine2, theirs2 = project(
        place, group, spans, gathered, [(weight_mid2, weight_end2)], cost=HEAVY
    )
    both2, arrived = together(summed(mine2, theirs2), arrived)
    turns = [
        lax.dynamic_index_in_dim(both2, jnp.bitwise_xor(j, turn), 0, keepdims=False)
        for turn in range(PLANE)
    ]
    turns = turns[:1] + [send(turns[turn], PLANE_SWAP[turn]) for turn in range(1, PLANE)]
    turns = [jnp.where(j % 2 == 1, turns[i ^ 1], turns[i]) for i in range(PLANE)]
    turns = [jnp.where(j >= 2, turns[i ^ 2], turns[i]) for i in range(PLANE)]
    out = place_rows(out, arrived, [z, jnp.bitwise_xor(z, 1), far])
    return place_rows(out, jnp.stack(turns), [jnp.bitwise_xor(far, 1)])


def solution(mesh):
    placed = (
        P("seq", "head"),
        P("seq", "head"),
        P("seq", "head"),
        P("head", "seq", None, None),
        P("seq", "head"),
    )

    def local(queries, *rest):
        heads_here = queries.shape[1] // HD
        two_level = (
            mesh.shape["seq"] == LINE * PLANE
            and mesh.shape["head"] == 2
            and heads_here % LINE == 0
        )
        return (two_level_plan if two_level else ring_plan)(queries, *rest)

    return jax.shard_map(
        local, mesh=mesh, in_specs=placed, out_specs=P(("seq", "head"), None), check_vma=False
    )
```

```python
import functools
import math

import jax
import jax.numpy as jnp
from jax import lax
from jax.experimental import pallas as pl
from jax.experimental.pallas import tpu as pltpu
from jax.sharding import PartitionSpec as P

HD = 128
CYCLE = 8
BLOCK = 128
LINE = 4
PLANE = 4
MASKED = -1e30
HEAVY = pl.CostEstimate(flops=10**10, bytes_accessed=2**24, transcendentals=0)
LIGHT = pl.CostEstimate(flops=1, bytes_accessed=1, transcendentals=0)


def feature_map(numbers):
    x = numbers.astype(jnp.float32)
    return jnp.where(x > 0, x + 1.0, jnp.exp(jnp.minimum(x, 0.0))).astype(jnp.bfloat16)


def passed_along(value, axis, steps):
    count = lax.axis_size(axis)
    pairs = [(source, (source + steps) % count) for source in range(count)]
    return lax.ppermute(value, axis, pairs)


def token_classes(block_row, tok_rows, key_rows):
    heads_here, query_blocks, key_blocks = block_row.shape
    query_width = tok_rows // query_blocks
    key_width = key_rows // key_blocks
    widened = jnp.broadcast_to(
        block_row[:, :, None, :, None],
        (heads_here, query_blocks, query_width, key_blocks, key_width),
    )
    return widened.reshape(heads_here, tok_rows, key_rows)


def ring_plan(queries, keys, values, class_map, out_weight):
    tok_rows = queries.shape[0]
    heads_here = queries.shape[1] // HD
    current = jnp.stack([keys, values])
    arrivals = [current]
    for _ in range(1, CYCLE):
        current = passed_along(current, "seq", 1)
        arrivals.append(current)
    window = jnp.concatenate(arrivals, axis=1)
    key_rows = window.shape[1]
    query_heads = queries.reshape(tok_rows, heads_here, HD)
    key_heads = window[0].reshape(key_rows, heads_here, HD)
    value_heads = window[1].reshape(key_rows, heads_here, HD)
    block_count = class_map.shape[1]
    classes = token_classes(class_map.reshape(heads_here, block_count, -1), tok_rows, key_rows)
    scores = jnp.einsum(
        "thd,uhd->htu", query_heads, key_heads, preferred_element_type=jnp.float32
    ) * (1.0 / math.sqrt(HD))
    masked = jnp.where(classes == 2, scores, -jnp.inf)
    row_max = jnp.max(masked, axis=2, keepdims=True)
    probs = jnp.exp(masked - row_max)
    exact_total = jnp.sum(probs, axis=2, keepdims=True)
    apply_values = functools.partial(
        jnp.einsum, "htu,uhd->htd", preferred_element_type=jnp.float32
    )
    exact_out = apply_values(probs.astype(jnp.bfloat16), value_heads) / exact_total
    affinity = jnp.einsum(
        "thd,uhd->htu",
        feature_map(query_heads),
        feature_map(key_heads),
        preferred_element_type=jnp.float32,
    )
    affinity = jnp.where(classes == 1, affinity, 0.0)
    linear_total = jnp.maximum(jnp.sum(affinity, axis=2, keepdims=True), 1.0)
    linear_out = apply_values(affinity.astype(jnp.bfloat16), value_heads) / linear_total
    attended = (
        (exact_out + linear_out)
        .transpose(1, 0, 2)
        .reshape(tok_rows, heads_here * HD)
        .astype(jnp.bfloat16)
    )
    partial_rows = lax.dot_general(
        attended,
        lax.all_gather(out_weight, "seq", axis=0, tiled=True),
        (((1,), (1,)), ((), ())),
        preferred_element_type=jnp.float32,
    )
    return lax.psum_scatter(
        partial_rows.astype(jnp.bfloat16), "head", scatter_dimension=0, tiled=True
    )


def moves(target):
    pairs = []
    for z in range(LINE):
        for j in range(PLANE):
            to = target(z, j)
            if to is not None:
                pairs.append((z * PLANE + j, to[0] * PLANE + to[1]))
    return pairs


PLANES = [[z * PLANE + j for j in range(PLANE)] for z in range(LINE)]
PLANE_SWAP = [moves(lambda z, j, turn=turn: (z, j ^ turn)) for turn in range(PLANE)]
NEXT_PLANE = moves(lambda z, j: ((z + 1) % LINE, j))
SWAP_PAIR = moves(lambda z, j: (z ^ 1, j))
SWAP_MID = moves(lambda z, j: (3 - z, j) if z in (1, 2) else None)
TO_ENDS = moves(lambda z, j: ({1: 0, 2: 3}[z], j) if z in (1, 2) else None)

CONTRACT_LAST = (((1,), (1,)), ((), ()))
CONTRACT_ROWS = (((1,), (0,)), ((), ()))
CONTRACT_FIRST = (((0,), (0,)), ((), ()))
SMEM = pl.BlockSpec(memory_space=pltpu.SMEM)
VMEM = pl.BlockSpec(memory_space=pltpu.VMEM)


def send(value, pairs):
    return lax.ppermute(value, "seq", pairs)


def exchange(value):
    return lax.all_to_all(value, "seq", 0, 0, tiled=True, axis_index_groups=PLANES)


def after(value, *others):
    return lax.optimization_barrier((value,) + others)[0]


def dot(left, right, dims):
    return lax.dot_general(left, right, dims, preferred_element_type=jnp.float32)


def together(*values):
    return lax.optimization_barrier(values)


def pack_kernel(group, count, *refs):
    out = refs[count]
    for owner in range(PLANE):
        for h in range(group):
            at = (owner * group + h) * HD
            for i in range(count):
                out[owner, h, i] = refs[i][:, at : at + HD]


def pack(group, *arrays):
    tok = arrays[0].shape[0]
    shape = (PLANE, group, len(arrays), tok, HD)
    return pl.pallas_call(
        functools.partial(pack_kernel, group, len(arrays)),
        out_shape=jax.ShapeDtypeStruct(shape, jnp.bfloat16),
        in_specs=[VMEM] * len(arrays),
        out_specs=VMEM,
        compiler_params=pltpu.CompilerParams(vmem_limit_bytes=24 * 1024 * 1024),
        cost_estimate=pl.CostEstimate(
            flops=0, bytes_accessed=4 * len(arrays) * arrays[0].size, transcendentals=0
        ),
    )(*arrays)


def attention_kernel(tok, q_ref, own, last, last2, bias_ref, lin_ref, out_ref, k_all, v_all, s_all):
    blocks = tok // BLOCK
    window = CYCLE * tok
    skipped = 2 * PLANE + 1 - CYCLE
    scale = math.log2(math.e) / math.sqrt(HD)

    @pl.when(pl.program_id(0) == 0)
    def _():
        v_all[:, HD:] = jnp.ones((v_all.shape[0], HD), jnp.bfloat16)

    def fill(ref, places, first):
        def body(i, carry):
            k, v = ref[i, 0, 0], ref[i, 0, 1]
            at = pl.multiple_of((first + i) * tok, tok)
            k_all[pl.ds(at, tok), :] = k
            v_all[pl.ds(at, tok), :HD] = v
            f = feature_map(k)
            counted = jnp.concatenate([v, jnp.ones_like(v)], axis=1)
            for b in range(blocks):
                block = slice(b * BLOCK, (b + 1) * BLOCK)
                s_all[pl.ds(at + b * BLOCK, BLOCK), :] = dot(
                    f[block], counted[block], CONTRACT_FIRST
                ).astype(jnp.bfloat16)
            return carry

        lax.fori_loop(0, places, body, 0, unroll=True)

    fill(last2, PLANE - skipped, 0)
    fill(last, PLANE, PLANE - skipped)
    fill(own, PLANE, 2 * PLANE - skipped)

    def one_shard(i, carry):
        rows = pl.ds(pl.multiple_of(i * tok, tok), window)
        q = q_ref[i, 0, 0]
        scores = dot(q, k_all[rows, :], CONTRACT_LAST)
        scores = scores.reshape(blocks, BLOCK, window) * scale + bias_ref[0, i][:, None, :]
        scores = scores.reshape(tok, window)
        probs = jnp.exp2(scores - jnp.max(scores, axis=1, keepdims=True))
        exact = dot(probs.astype(jnp.bfloat16), v_all[rows, :], CONTRACT_ROWS)
        f = jnp.concatenate([feature_map(q)] * (window // BLOCK), axis=1)
        f = (f.reshape(blocks, BLOCK, window) * lin_ref[0, i][:, None, :]).reshape(tok, window)
        linear = dot(f, s_all[rows, :], CONTRACT_ROWS)
        out_ref[i, 0] = (
            exact[:, :HD] / exact[:, HD:] + linear[:, :HD] / jnp.maximum(linear[:, HD:], 1.0)
        ).astype(jnp.bfloat16)
        return carry

    lax.fori_loop(0, PLANE, one_shard, 0, unroll=2)


def attention(first, count, q, own, last, last2, bias, lin):
    tok = q.shape[3]
    rows = (2 * PLANE + last2.shape[0]) * tok
    pairs = count * tok * PLANE * CYCLE * tok

    def heads(array, start):
        shape = array.shape[:1] + (1,) + array.shape[2:]
        zeros = (0,) * (array.ndim - 2)
        return pl.BlockSpec(shape, lambda h: (0, start + h) + zeros)

    def masks(array):
        return pl.BlockSpec((1,) + array.shape[1:], lambda h: (first + h, 0, 0, 0))

    return pl.pallas_call(
        functools.partial(attention_kernel, tok),
        grid=(count,),
        out_shape=jax.ShapeDtypeStruct((PLANE, count, tok, HD), jnp.bfloat16),
        in_specs=[heads(q, first), heads(own, first), heads(last, first), heads(last2, 0)]
        + [masks(bias), masks(lin)],
        out_specs=pl.BlockSpec((PLANE, 1, tok, HD), lambda h: (0, h, 0, 0)),
        scratch_shapes=[
            pltpu.VMEM((rows, HD), jnp.bfloat16),
            pltpu.VMEM((rows, 2 * HD), jnp.bfloat16),
            pltpu.VMEM((rows, 2 * HD), jnp.bfloat16),
        ],
        compiler_params=pltpu.CompilerParams(vmem_limit_bytes=48 * 1024 * 1024),
        cost_estimate=pl.CostEstimate(
            flops=8 * pairs * HD, bytes_accessed=8 * count * rows * HD, transcendentals=pairs
        ),
    )(q, own, last, last2, bias, lin)


def project_kernel(tok, group, spans, summed, begun, ends, place, *refs):
    j, core = place[1], place[2]
    sources = refs[: PLANE * len(spans)]
    refs = refs[PLANE * len(spans) :]
    pieces = []
    for two in summed:
        pieces.append(refs[: 1 + two])
        refs = refs[1 + two :]
    so_far = refs[0] if begun else None
    *outs, left, weight = refs[1 if begun else 0 :]
    blocks = []
    base = 0
    for g, (first, count) in enumerate(spans):
        width = count * HD
        for turn in range(PLANE):
            owner = jnp.bitwise_xor(j, turn)
            for h in range(count):
                lanes = pl.ds(pl.multiple_of(base + owner * width + h * HD, HD), HD)
                for i in range(PLANE):
                    left[i * tok : (i + 1) * tok, lanes] = sources[PLANE * g + turn][i, h]
        for owner in range(PLANE):
            there = (owner * group + first) * HD
            blocks.append((base + owner * width, there, width))
        base += PLANE * width

    for p, piece in enumerate(pieces):
        if len(piece) == 2:
            weight[...] = piece[0][...] + piece[1][...]
            source = weight
        else:
            source = piece[0]

        def one_shard(i, carry, p=p, source=source):
            rows = pl.ds(pl.multiple_of(i * tok, tok), tok)
            product = so_far[i, p] if begun else None
            for here, there, width in blocks:
                term = dot(
                    source[:, there : there + width], left[rows, here : here + width], CONTRACT_LAST
                )
                product = term if product is None else product + term
            if not ends:
                outs[0][i, p] = product
                return carry
            product = product.astype(jnp.bfloat16)
            low, high = product[:, : tok // 2], product[:, tok // 2 :]
            outs[0][i, p] = jnp.where(core == 0, low, high)
            outs[1][i, p] = jnp.where(core == 0, high, low)
            return carry

        lax.fori_loop(0, PLANE, one_shard, 0, unroll=2)


def project(place, group, spans, gathered, pieces, so_far=None, ends=True, cost=LIGHT):
    tok = gathered[0].shape[2]
    rows, depth = pieces[0][0].shape
    operands = [*gathered] + [a for piece in pieces for a in piece]
    if so_far is not None:
        operands.append(so_far)
    if ends:
        outs = [jax.ShapeDtypeStruct((PLANE, len(pieces), rows, tok // 2), jnp.bfloat16)] * 2
    else:
        outs = [jax.ShapeDtypeStruct((PLANE, len(pieces), rows, tok), jnp.float32)]
    some = sum(count for _, count in spans) * PLANE * HD
    return pl.pallas_call(
        functools.partial(
            project_kernel,
            tok,
            group,
            spans,
            tuple(len(p) - 1 for p in pieces),
            so_far is not None,
            ends,
        ),
        out_shape=outs,
        in_specs=[SMEM] + [VMEM] * len(operands),
        out_specs=[VMEM] * len(outs),
        scratch_shapes=[
            pltpu.VMEM((PLANE * tok, some), jnp.bfloat16),
            pltpu.VMEM((rows, depth), jnp.bfloat16),
        ],
        compiler_params=pltpu.CompilerParams(vmem_limit_bytes=48 * 1024 * 1024),
        cost_estimate=cost,
    )(place, *operands)


def two_level_plan(queries, keys, values, class_map, out_weight):
    tok = queries.shape[0]
    heads = queries.shape[1] // HD
    group = heads // PLANE
    early = max(1, 3 * group // 5)
    spans = ((0, early), (early, group - early))
    here = lax.axis_index("seq")
    core = lax.axis_index("head")
    z, j = here // PLANE, here % PLANE
    place = jnp.stack([z, j, core]).astype(jnp.int32)
    skipped = 2 * PLANE + 1 - CYCLE

    packed = pack(group, keys, values)
    weight_pair = send(out_weight, SWAP_PAIR)
    weight_mid = send(out_weight, SWAP_MID)
    own, queries, weight_pair, weight_mid = together(
        exchange(packed), queries, weight_pair, weight_mid
    )

    q = exchange(pack(group, queries))
    last = send(own, NEXT_PLANE)
    parts = after(class_map, own).reshape((PLANE, group) + class_map.shape[1:])
    class_parts = []
    for turn in range(PLANE):
        part = lax.dynamic_index_in_dim(parts, jnp.bitwise_xor(j, turn), 0, keepdims=False)
        class_parts.append(send(part, PLANE_SWAP[turn]) if turn else part)
    class_parts = [
        jnp.where(j % 2 == 1, class_parts[i ^ 1], class_parts[i]) for i in range(PLANE)
    ]
    class_parts = [jnp.where(j >= 2, class_parts[i ^ 2], class_parts[i]) for i in range(PLANE)]
    classes = jnp.stack(class_parts, axis=1)[:, :, :, ::-1, :]
    classes = classes.reshape(classes.shape[:3] + (-1, 1))
    wide = jnp.broadcast_to(classes, classes.shape[:4] + (BLOCK,)).reshape(classes.shape[:3] + (-1,))
    bias = jnp.where(wide == 2, 0.0, MASKED).astype(jnp.float32)
    lin = jnp.where(wide == 1, 1.0, 0.0).astype(jnp.bfloat16)

    q, own, last, bias, lin, weight_pair, weight_mid = together(
        q, own, last, bias, lin, weight_pair, weight_mid
    )

    behind = last[skipped:]
    last2 = send(behind[:, :early], NEXT_PLANE)
    late2 = send(after(behind[:, early:], last2), NEXT_PLANE)
    att = attention(0, early, q, own, last, last2, bias, lin)
    q, own, last, late2, att, bias, lin, weight_pair, weight_mid = together(
        q, own, last, late2, att, bias, lin, weight_pair, weight_mid
    )

    weight_end = send(weight_mid, TO_ENDS)
    weight_mid2 = send(weight_pair, SWAP_MID)
    gathered = [att] + [send(att, PLANE_SWAP[turn]) for turn in range(1, PLANE)]
    late = attention(early, group - early, q, own, last, late2, bias, lin)
    late, weight_pair, weight_mid, weight_end, weight_mid2, *gathered = together(
        late, weight_pair, weight_mid, weight_end, weight_mid2, *gathered
    )

    weight_end2 = send(weight_mid2, TO_ENDS)
    gathered += [late] + [send(late, PLANE_SWAP[turn]) for turn in range(1, PLANE)]
    far = jnp.where(z < 2, 2, 1)
    rows = out_weight.shape[0]
    out = jnp.zeros((tok // 2, LINE * PLANE * rows), jnp.bfloat16)

    def summed(mine, theirs):
        other = lax.ppermute(theirs, "head", [(0, 1), (1, 0)])
        return (mine.astype(jnp.float32) + other.astype(jnp.float32)).astype(jnp.bfloat16)

    def place_rows(out, arrived, lines):
        for p, line in enumerate(lines):
            wide = arrived[:, p].reshape(PLANE * rows, tok // 2).T
            out = lax.dynamic_update_slice_in_dim(out, wide, line * PLANE * rows, 1)
        return out

    pieces = [(out_weight,), (weight_pair,), (weight_mid, weight_end)]
    (so_far,) = project(place, group, spans[:1], gathered[:PLANE], pieces, ends=False)
    mine, theirs = project(place, group, spans[1:], gathered[PLANE:], pieces, so_far)
    mine, theirs, *gathered = together(mine, theirs, *gathered)

    both, weight_mid2, weight_end2 = together(summed(mine, theirs), weight_mid2, weight_end2)
    arrived = exchange(both)
    mine2, theirs2 = project(
        place, group, spans, gathered, [(weight_mid2, weight_end2)], cost=HEAVY
    )
    both2, arrived = together(summed(mine2, theirs2), arrived)
    turns = [
        lax.dynamic_index_in_dim(both2, jnp.bitwise_xor(j, turn), 0, keepdims=False)
        for turn in range(PLANE)
    ]
    turns = turns[:1] + [send(turns[turn], PLANE_SWAP[turn]) for turn in range(1, PLANE)]
    turns = [jnp.where(j % 2 == 1, turns[i ^ 1], turns[i]) for i in range(PLANE)]
    turns = [jnp.where(j >= 2, turns[i ^ 2], turns[i]) for i in range(PLANE)]
    out = place_rows(out, arrived, [z, jnp.bitwise_xor(z, 1), far])
    return place_rows(out, jnp.stack(turns), [jnp.bitwise_xor(far, 1)])


def solution(mesh):
    placed = (
        P("seq", "head"),
        P("seq", "head"),
        P("seq", "head"),
        P("head", "seq", None, None),
        P("seq", "head"),
    )

    def local(queries, *rest):
        heads_here = queries.shape[1] // HD
        two_level = (
            mesh.shape["seq"] == LINE * PLANE
            and mesh.shape["head"] == 2
            and heads_here % LINE == 0
        )
        return (two_level_plan if two_level else ring_plan)(queries, *rest)

    return jax.shard_map(
        local, mesh=mesh, in_specs=placed, out_specs=P(("seq", "head"), None), check_vma=False
    )
```

```python
import functools
import math

import jax
import jax.numpy as jnp
from jax import lax
from jax.experimental import pallas as pl
from jax.experimental.pallas import tpu as pltpu
from jax.sharding import PartitionSpec as P

HD = 128
CYCLE = 8
BLOCK = 128
LINE = 4
PLANE = 4
MASKED = -1e30
HEAVY = pl.CostEstimate(flops=10**10, bytes_accessed=2**24, transcendentals=0)
LIGHT = pl.CostEstimate(flops=1, bytes_accessed=1, transcendentals=0)


def feature_map(numbers):
    x = numbers.astype(jnp.float32)
    return jnp.where(x > 0, x + 1.0, jnp.exp(jnp.minimum(x, 0.0))).astype(jnp.bfloat16)


def passed_along(value, axis, steps):
    count = lax.axis_size(axis)
    pairs = [(source, (source + steps) % count) for source in range(count)]
    return lax.ppermute(value, axis, pairs)


def token_classes(block_row, tok_rows, key_rows):
    heads_here, query_blocks, key_blocks = block_row.shape
    query_width = tok_rows // query_blocks
    key_width = key_rows // key_blocks
    widened = jnp.broadcast_to(
        block_row[:, :, None, :, None],
        (heads_here, query_blocks, query_width, key_blocks, key_width),
    )
    return widened.reshape(heads_here, tok_rows, key_rows)


def ring_plan(queries, keys, values, class_map, out_weight):
    tok_rows = queries.shape[0]
    heads_here = queries.shape[1] // HD
    current = jnp.stack([keys, values])
    arrivals = [current]
    for _ in range(1, CYCLE):
        current = passed_along(current, "seq", 1)
        arrivals.append(current)
    window = jnp.concatenate(arrivals, axis=1)
    key_rows = window.shape[1]
    query_heads = queries.reshape(tok_rows, heads_here, HD)
    key_heads = window[0].reshape(key_rows, heads_here, HD)
    value_heads = window[1].reshape(key_rows, heads_here, HD)
    block_count = class_map.shape[1]
    classes = token_classes(class_map.reshape(heads_here, block_count, -1), tok_rows, key_rows)
    scores = jnp.einsum(
        "thd,uhd->htu", query_heads, key_heads, preferred_element_type=jnp.float32
    ) * (1.0 / math.sqrt(HD))
    masked = jnp.where(classes == 2, scores, -jnp.inf)
    row_max = jnp.max(masked, axis=2, keepdims=True)
    probs = jnp.exp(masked - row_max)
    exact_total = jnp.sum(probs, axis=2, keepdims=True)
    apply_values = functools.partial(
        jnp.einsum, "htu,uhd->htd", preferred_element_type=jnp.float32
    )
    exact_out = apply_values(probs.astype(jnp.bfloat16), value_heads) / exact_total
    affinity = jnp.einsum(
        "thd,uhd->htu",
        feature_map(query_heads),
        feature_map(key_heads),
        preferred_element_type=jnp.float32,
    )
    affinity = jnp.where(classes == 1, affinity, 0.0)
    linear_total = jnp.maximum(jnp.sum(affinity, axis=2, keepdims=True), 1.0)
    linear_out = apply_values(affinity.astype(jnp.bfloat16), value_heads) / linear_total
    attended = (
        (exact_out + linear_out)
        .transpose(1, 0, 2)
        .reshape(tok_rows, heads_here * HD)
        .astype(jnp.bfloat16)
    )
    partial_rows = lax.dot_general(
        attended,
        lax.all_gather(out_weight, "seq", axis=0, tiled=True),
        (((1,), (1,)), ((), ())),
        preferred_element_type=jnp.float32,
    )
    return lax.psum_scatter(
        partial_rows.astype(jnp.bfloat16), "head", scatter_dimension=0, tiled=True
    )


def moves(target):
    pairs = []
    for z in range(LINE):
        for j in range(PLANE):
            to = target(z, j)
            if to is not None:
                pairs.append((z * PLANE + j, to[0] * PLANE + to[1]))
    return pairs


PLANES = [[z * PLANE + j for j in range(PLANE)] for z in range(LINE)]
PLANE_SWAP = [moves(lambda z, j, turn=turn: (z, j ^ turn)) for turn in range(PLANE)]
NEXT_PLANE = moves(lambda z, j: ((z + 1) % LINE, j))
SWAP_PAIR = moves(lambda z, j: (z ^ 1, j))
SWAP_MID = moves(lambda z, j: (3 - z, j) if z in (1, 2) else None)
TO_ENDS = moves(lambda z, j: ({1: 0, 2: 3}[z], j) if z in (1, 2) else None)

CONTRACT_LAST = (((1,), (1,)), ((), ()))
CONTRACT_ROWS = (((1,), (0,)), ((), ()))
CONTRACT_FIRST = (((0,), (0,)), ((), ()))
SMEM = pl.BlockSpec(memory_space=pltpu.SMEM)
VMEM = pl.BlockSpec(memory_space=pltpu.VMEM)


def send(value, pairs):
    return lax.ppermute(value, "seq", pairs)


def exchange(value):
    return lax.all_to_all(value, "seq", 0, 0, tiled=True, axis_index_groups=PLANES)


def after(value, *others):
    return lax.optimization_barrier((value,) + others)[0]


def dot(left, right, dims):
    return lax.dot_general(left, right, dims, preferred_element_type=jnp.float32)


def together(*values):
    return lax.optimization_barrier(values)


def pack_kernel(group, count, *refs):
    out = refs[count]
    for owner in range(PLANE):
        for h in range(group):
            at = (owner * group + h) * HD
            for i in range(count):
                out[owner, h, i] = refs[i][:, at : at + HD]


def pack(group, *arrays):
    tok = arrays[0].shape[0]
    shape = (PLANE, group, len(arrays), tok, HD)
    return pl.pallas_call(
        functools.partial(pack_kernel, group, len(arrays)),
        out_shape=jax.ShapeDtypeStruct(shape, jnp.bfloat16),
        in_specs=[VMEM] * len(arrays),
        out_specs=VMEM,
        compiler_params=pltpu.CompilerParams(vmem_limit_bytes=24 * 1024 * 1024),
        cost_estimate=pl.CostEstimate(
            flops=0, bytes_accessed=4 * len(arrays) * arrays[0].size, transcendentals=0
        ),
    )(*arrays)


def attention_kernel(tok, q_ref, own, last, last2, bias_ref, lin_ref, out_ref, k_all, v_all, s_all):
    blocks = tok // BLOCK
    window = CYCLE * tok
    skipped = 2 * PLANE + 1 - CYCLE
    scale = math.log2(math.e) / math.sqrt(HD)

    @pl.when(pl.program_id(0) == 0)
    def _():
        v_all[:, HD:] = jnp.ones((v_all.shape[0], HD), jnp.bfloat16)

    def fill(ref, places, first):
        def body(i, carry):
            k, v = ref[i, 0, 0], ref[i, 0, 1]
            at = pl.multiple_of((first + i) * tok, tok)
            k_all[pl.ds(at, tok), :] = k
            v_all[pl.ds(at, tok), :HD] = v
            f = feature_map(k)
            counted = jnp.concatenate([v, jnp.ones_like(v)], axis=1)
            for b in range(blocks):
                block = slice(b * BLOCK, (b + 1) * BLOCK)
                s_all[pl.ds(at + b * BLOCK, BLOCK), :] = dot(
                    f[block], counted[block], CONTRACT_FIRST
                ).astype(jnp.bfloat16)
            return carry

        lax.fori_loop(0, places, body, 0, unroll=True)

    fill(last2, PLANE - skipped, 0)
    fill(last, PLANE, PLANE - skipped)
    fill(own, PLANE, 2 * PLANE - skipped)

    def one_shard(i, carry):
        rows = pl.ds(pl.multiple_of(i * tok, tok), window)
        q = q_ref[i, 0, 0]
        scores = dot(q, k_all[rows, :], CONTRACT_LAST)
        scores = scores.reshape(blocks, BLOCK, window) * scale + bias_ref[0, i][:, None, :]
        scores = scores.reshape(tok, window)
        probs = jnp.exp2(scores - jnp.max(scores, axis=1, keepdims=True))
        exact = dot(probs.astype(jnp.bfloat16), v_all[rows, :], CONTRACT_ROWS)
        f = jnp.concatenate([feature_map(q)] * (window // BLOCK), axis=1)
        f = (f.reshape(blocks, BLOCK, window) * lin_ref[0, i][:, None, :]).reshape(tok, window)
        linear = dot(f, s_all[rows, :], CONTRACT_ROWS)
        out_ref[i, 0] = (
            exact[:, :HD] / exact[:, HD:] + linear[:, :HD] / jnp.maximum(linear[:, HD:], 1.0)
        ).astype(jnp.bfloat16)
        return carry

    lax.fori_loop(0, PLANE, one_shard, 0, unroll=2)


def attention(first, count, q, own, last, last2, bias, lin):
    tok = q.shape[3]
    rows = (2 * PLANE + last2.shape[0]) * tok
    pairs = count * tok * PLANE * CYCLE * tok

    def heads(array, start):
        shape = array.shape[:1] + (1,) + array.shape[2:]
        zeros = (0,) * (array.ndim - 2)
        return pl.BlockSpec(shape, lambda h: (0, start + h) + zeros)

    def masks(array):
        return pl.BlockSpec((1,) + array.shape[1:], lambda h: (first + h, 0, 0, 0))

    return pl.pallas_call(
        functools.partial(attention_kernel, tok),
        grid=(count,),
        out_shape=jax.ShapeDtypeStruct((PLANE, count, tok, HD), jnp.bfloat16),
        in_specs=[heads(q, first), heads(own, first), heads(last, first), heads(last2, 0)]
        + [masks(bias), masks(lin)],
        out_specs=pl.BlockSpec((PLANE, 1, tok, HD), lambda h: (0, h, 0, 0)),
        scratch_shapes=[
            pltpu.VMEM((rows, HD), jnp.bfloat16),
            pltpu.VMEM((rows, 2 * HD), jnp.bfloat16),
            pltpu.VMEM((rows, 2 * HD), jnp.bfloat16),
        ],
        compiler_params=pltpu.CompilerParams(vmem_limit_bytes=48 * 1024 * 1024),
        cost_estimate=pl.CostEstimate(
            flops=8 * pairs * HD, bytes_accessed=8 * count * rows * HD, transcendentals=pairs
        ),
    )(q, own, last, last2, bias, lin)


def project_kernel(tok, group, spans, summed, begun, ends, place, *refs):
    j, core = place[1], place[2]
    sources = refs[: PLANE * len(spans)]
    refs = refs[PLANE * len(spans) :]
    pieces = []
    for two in summed:
        pieces.append(refs[: 1 + two])
        refs = refs[1 + two :]
    so_far = refs[0] if begun else None
    *outs, left, weight = refs[1 if begun else 0 :]
    blocks = []
    base = 0
    for g, (first, count) in enumerate(spans):
        width = count * HD
        for turn in range(PLANE):
            owner = jnp.bitwise_xor(j, turn)
            for h in range(count):
                lanes = pl.ds(pl.multiple_of(base + owner * width + h * HD, HD), HD)
                for i in range(PLANE):
                    left[i * tok : (i + 1) * tok, lanes] = sources[PLANE * g + turn][i, h]
        for owner in range(PLANE):
            there = (owner * group + first) * HD
            blocks.append((base + owner * width, there, width))
        base += PLANE * width

    for p, piece in enumerate(pieces):
        if len(piece) == 2:
            weight[...] = piece[0][...] + piece[1][...]
            source = weight
        else:
            source = piece[0]

        def one_shard(i, carry, p=p, source=source):
            rows = pl.ds(pl.multiple_of(i * tok, tok), tok)
            product = so_far[i, p] if begun else None
            for here, there, width in blocks:
                term = dot(
                    source[:, there : there + width], left[rows, here : here + width], CONTRACT_LAST
                )
                product = term if product is None else product + term
            if not ends:
                outs[0][i, p] = product
                return carry
            product = product.astype(jnp.bfloat16)
            low, high = product[:, : tok // 2], product[:, tok // 2 :]
            outs[0][i, p] = jnp.where(core == 0, low, high)
            outs[1][i, p] = jnp.where(core == 0, high, low)
            return carry

        lax.fori_loop(0, PLANE, one_shard, 0, unroll=2)


def project(place, group, spans, gathered, pieces, so_far=None, ends=True, cost=LIGHT):
    tok = gathered[0].shape[2]
    rows, depth = pieces[0][0].shape
    operands = [*gathered] + [a for piece in pieces for a in piece]
    if so_far is not None:
        operands.append(so_far)
    if ends:
        outs = [jax.ShapeDtypeStruct((PLANE, len(pieces), rows, tok // 2), jnp.bfloat16)] * 2
    else:
        outs = [jax.ShapeDtypeStruct((PLANE, len(pieces), rows, tok), jnp.float32)]
    some = sum(count for _, count in spans) * PLANE * HD
    return pl.pallas_call(
        functools.partial(
            project_kernel,
            tok,
            group,
            spans,
            tuple(len(p) - 1 for p in pieces),
            so_far is not None,
            ends,
        ),
        out_shape=outs,
        in_specs=[SMEM] + [VMEM] * len(operands),
        out_specs=[VMEM] * len(outs),
        scratch_shapes=[
            pltpu.VMEM((PLANE * tok, some), jnp.bfloat16),
            pltpu.VMEM((rows, depth), jnp.bfloat16),
        ],
        compiler_params=pltpu.CompilerParams(vmem_limit_bytes=48 * 1024 * 1024),
        cost_estimate=cost,
    )(place, *operands)


def two_level_plan(queries, keys, values, class_map, out_weight):
    tok = queries.shape[0]
    heads = queries.shape[1] // HD
    group = heads // PLANE
    early = max(1, 3 * group // 5)
    spans = ((0, early), (early, group - early))
    here = lax.axis_index("seq")
    core = lax.axis_index("head")
    z, j = here // PLANE, here % PLANE
    place = jnp.stack([z, j, core]).astype(jnp.int32)
    skipped = 2 * PLANE + 1 - CYCLE

    packed = pack(group, keys, values)
    weight_pair = send(out_weight, SWAP_PAIR)
    weight_mid = send(out_weight, SWAP_MID)
    own, queries, weight_pair, weight_mid = together(
        exchange(packed), queries, weight_pair, weight_mid
    )

    q = exchange(pack(group, queries))
    last = send(own, NEXT_PLANE)
    parts = after(class_map, own).reshape((PLANE, group) + class_map.shape[1:])
    class_parts = []
    for turn in range(PLANE):
        part = lax.dynamic_index_in_dim(parts, jnp.bitwise_xor(j, turn), 0, keepdims=False)
        class_parts.append(send(part, PLANE_SWAP[turn]) if turn else part)
    class_parts = [
        jnp.where(j % 2 == 1, class_parts[i ^ 1], class_parts[i]) for i in range(PLANE)
    ]
    class_parts = [jnp.where(j >= 2, class_parts[i ^ 2], class_parts[i]) for i in range(PLANE)]
    classes = jnp.stack(class_parts, axis=1)[:, :, :, ::-1, :]
    classes = classes.reshape(classes.shape[:3] + (-1, 1))
    wide = jnp.broadcast_to(classes, classes.shape[:4] + (BLOCK,)).reshape(classes.shape[:3] + (-1,))
    bias = jnp.where(wide == 2, 0.0, MASKED).astype(jnp.float32)
    lin = jnp.where(wide == 1, 1.0, 0.0).astype(jnp.bfloat16)

    q, own, last, bias, lin, weight_pair, weight_mid = together(
        q, own, last, bias, lin, weight_pair, weight_mid
    )

    behind = last[skipped:]
    last2 = send(behind[:, :early], NEXT_PLANE)
    late2 = send(after(behind[:, early:], last2), NEXT_PLANE)
    att = attention(0, early, q, own, last, last2, bias, lin)
    q, own, last, late2, att, bias, lin, weight_pair, weight_mid = together(
        q, own, last, late2, att, bias, lin, weight_pair, weight_mid
    )

    weight_end = send(weight_mid, TO_ENDS)
    weight_mid2 = send(weight_pair, SWAP_MID)
    gathered = [att] + [send(att, PLANE_SWAP[turn]) for turn in range(1, PLANE)]
    late = attention(early, group - early, q, own, last, late2, bias, lin)
    late, weight_pair, weight_mid, weight_end, weight_mid2, *gathered = together(
        late, weight_pair, weight_mid, weight_end, weight_mid2, *gathered
    )

    weight_end2 = send(weight_mid2, TO_ENDS)
    gathered += [late] + [send(late, PLANE_SWAP[turn]) for turn in range(1, PLANE)]
    far = jnp.where(z < 2, 2, 1)
    rows = out_weight.shape[0]
    out = jnp.zeros((tok // 2, LINE * PLANE * rows), jnp.bfloat16)

    def summed(mine, theirs):
        other = lax.ppermute(theirs, "head", [(0, 1), (1, 0)])
        return (mine.astype(jnp.float32) + other.astype(jnp.float32)).astype(jnp.bfloat16)

    def place_rows(out, arrived, lines):
        for p, line in enumerate(lines):
            wide = arrived[:, p].reshape(PLANE * rows, tok // 2).T
            out = lax.dynamic_update_slice_in_dim(out, wide, line * PLANE * rows, 1)
        return out

    pieces = [(out_weight,), (weight_pair,), (weight_mid, weight_end)]
    (so_far,) = project(place, group, spans[:1], gathered[:PLANE], pieces, ends=False)
    mine, theirs = project(place, group, spans[1:], gathered[PLANE:], pieces, so_far)

    both, weight_mid2, weight_end2 = together(summed(mine, theirs), weight_mid2, weight_end2)
    arrived = exchange(both)
    mine2, theirs2 = project(
        place, group, spans, gathered, [(weight_mid2, weight_end2)], cost=HEAVY
    )
    both2, arrived = together(summed(mine2, theirs2), arrived)
    turns = [
        lax.dynamic_index_in_dim(both2, jnp.bitwise_xor(j, turn), 0, keepdims=False)
        for turn in range(PLANE)
    ]
    turns = turns[:1] + [send(turns[turn], PLANE_SWAP[turn]) for turn in range(1, PLANE)]
    turns = [jnp.where(j % 2 == 1, turns[i ^ 1], turns[i]) for i in range(PLANE)]
    turns = [jnp.where(j >= 2, turns[i ^ 2], turns[i]) for i in range(PLANE)]
    out = place_rows(out, arrived, [z, jnp.bitwise_xor(z, 1), far])
    return place_rows(out, jnp.stack(turns), [jnp.bitwise_xor(far, 1)])


def solution(mesh):
    placed = (
        P("seq", "head"),
        P("seq", "head"),
        P("seq", "head"),
        P("head", "seq", None, None),
        P("seq", "head"),
    )

    def local(queries, *rest):
        heads_here = queries.shape[1] // HD
        two_level = (
            mesh.shape["seq"] == LINE * PLANE
            and mesh.shape["head"] == 2
            and heads_here % LINE == 0
        )
        return (two_level_plan if two_level else ring_plan)(queries, *rest)

    return jax.shard_map(
        local, mesh=mesh, in_specs=placed, out_specs=P(("seq", "head"), None), check_vma=False
    )
```
